32 devices in a mesh: tm: 4 (over y, x), space: 8 (over z, core).
Axes of the slice: x: 2, y: 2, z: 4, core: 2. Of those that a mesh axis runs over, the one named last changes fastest.
Arguments:
- potential: float32 [64, 64, 128, 128], P('tm', 'space'), may hold values from -6 to 6
- multiplier: float32 [4, 64, 64, 128, 128], P(None, 'tm', 'space'), may hold values from -12 to 12
- start_density: float32 [64, 128, 128], P('space'), may hold values from 0.1 to 1
- final_density: float32 [64, 128, 128], P('space'), may hold values from 0.1 to 1
Outputs:
- next_potential: float32 [64, 64, 128, 128], P('tm', 'space')
- next_multiplier: float32 [4, 64, 64, 128, 128], P(None, 'tm', 'space')
The draws below stay inside these ranges and needn't reach their ends.
All inputs are finite; a program needn't handle non-finite values.
Results may differ from the reference program's by a relative error of at most 0.0003.
Values sent between devices are 32-bit elements; how exact they have to be, the bound alone decides.
No kernel may reach another device: no remote copies, remote signals or barrier semaphores. Data moves between devices by JAX's collectives and lax.ppermute only.
A program may use at most 256 MiB of HBM per device.

```python
import math
import jax
import jax.numpy as jnp
from jax import lax

NT = 64
NX = 64
NY = 128
NZ = 128
NEWTON = 10


def level_of(stream_key, extent, shards, smallest, top_value):
    def one(position, blocks):
        steps = jax.random.uniform(jax.random.fold_in(jax.random.fold_in(stream_key, 6), position), (blocks,), jnp.float32, smallest / len(shards), top_value / len(shards))
        return jnp.repeat(jnp.exp(steps), extent[position] // blocks).reshape((-1,) + (1,) * (len(extent) - position - 1))

    level = one(*shards[0])
    for cut in shards[1:]:
        level = level * one(*cut)
    return level


def normal_values(rng, extent, scale, reach, shards=(), kind=jnp.bfloat16):
    drawn = scale * jax.random.normal(rng, extent, jnp.float32)
    if shards:
        drawn = drawn * level_of(rng, extent, shards, -0.22, 0.18)
    return jnp.clip(drawn, -reach, reach).astype(kind)


def setup_inputs(seed: int = 0) -> dict:
    keys = jax.random.split(jax.random.key(seed), 5)
    potential = normal_values(keys[0], (NT, NX, NY, NZ), 1.0, 6.0, ((0, 4), (1, 8)), jnp.float32)
    multiplier = normal_values(keys[1], (4, NT, NX, NY, NZ), 2.0, 12.0, ((1, 4), (2, 8)), jnp.float32)
    start_density = jnp.clip(jnp.exp(math.log(1.0) - 2.3025851 * jax.random.uniform(keys[2], (NX, NY, NZ), jnp.float32) ** level_of(keys[2], (NX, NY, NZ), ((0, 8),), -0.2, 0.2)), 0.1, 1.0)
    final_density = jnp.clip(jnp.exp(math.log(1.0) - 2.3025851 * jax.random.uniform(keys[3], (NX, NY, NZ), jnp.float32) ** level_of(keys[3], (NX, NY, NZ), ((0, 8),), -0.2, 0.2)), 0.1, 1.0)
    return dict(potential=potential, multiplier=multiplier, start_density=start_density, final_density=final_density)


RATE = 4.0
PROX = 0.01

def cosine_table(length):
    freq = jnp.arange(length, dtype=jnp.float32)[:, None]
    place = jnp.arange(length, dtype=jnp.float32)[None, :]
    weight = jnp.where(freq == 0.0, jnp.sqrt(jnp.float32(0.5)), jnp.float32(1.0))
    return jnp.sqrt(jnp.float32(2.0) / length) * weight * jnp.cos(jnp.pi * freq * (place + 0.5) / length)

def eigen(length):
    freq = jnp.arange(length, dtype=jnp.float32)
    return 4.0 * jnp.square(jnp.sin(jnp.pi * freq / (2.0 * length)))

def forward_diff(field, axis):
    size = field.shape[axis]
    upper = lax.slice_in_dim(field, 1, size, axis=axis)
    lower = lax.slice_in_dim(field, 0, size - 1, axis=axis)
    edge = jnp.zeros_like(lax.slice_in_dim(field, 0, 1, axis=axis))
    return jnp.concatenate([upper - lower, edge], axis=axis)

def adjoint(face, axis):
    size = face.shape[axis]
    inner = lax.slice_in_dim(face, 0, size - 1, axis=axis)
    edge = jnp.zeros_like(lax.slice_in_dim(face, 0, 1, axis=axis))
    return jnp.concatenate([edge, inner], axis=axis) - jnp.concatenate([inner, edge], axis=axis)

def project(target):
    lead = target[0]
    side = target[1:]
    wsq = lax.optimization_barrier(jnp.sum(side * side, axis=0))
    excess = lead + 0.5 * wsq
    stretch = jnp.maximum(1.0, lead + 1.0)
    for step in range(NEWTON):
        resid = stretch - (lead + 1.0) - 0.5 * wsq / (stretch * stretch)
        slope = 1.0 + wsq / (stretch * stretch * stretch)
        stretch = jnp.maximum(1.0, stretch - resid / slope)
    inside = excess <= 0.0
    new_lead = jnp.where(inside, lead, lead - (stretch - 1.0))
    new_side = jnp.where(inside[None], side, side / stretch[None])
    return jnp.concatenate([new_lead[None], new_side], axis=0)

def reference(potential, multiplier, start_density, final_density):
    high = lax.Precision.HIGHEST
    gradient = jnp.stack([forward_diff(potential, axis) for axis in range(4)])
    projected = project(gradient + multiplier / RATE)
    next_multiplier = multiplier + RATE * (gradient - projected)
    flux = next_multiplier - RATE * projected
    right_side = -(adjoint(flux[0], 0) + adjoint(flux[1], 1) + adjoint(flux[2], 2) + adjoint(flux[3], 3))
    right_side = right_side + PROX * potential
    right_side = right_side.at[0].add(start_density)
    right_side = right_side.at[NT - 1].add(-final_density)
    cos_t = cosine_table(NT)
    cos_x = cosine_table(NX)
    cos_y = cosine_table(NY)
    cos_z = cosine_table(NZ)
    hat = jnp.einsum('ki,ixyz->kxyz', cos_t, right_side, precision=high)
    hat = jnp.einsum('ki,tiyz->tkyz', cos_x, hat, precision=high)
    hat = jnp.einsum('ki,txiz->txkz', cos_y, hat, precision=high)
    hat = jnp.einsum('ki,txyi->txyk', cos_z, hat, precision=high)
    denom = eigen(NT)[:, None, None, None] + eigen(NX)[None, :, None, None]
    denom = denom + eigen(NY)[None, None, :, None] + eigen(NZ)[None, None, None, :]
    hat = hat / (RATE * denom + PROX)
    hat = jnp.einsum('ik,kxyz->ixyz', cos_t, hat, precision=high)
    hat = jnp.einsum('ik,tkyz->tiyz', cos_x, hat, precision=high)
    hat = jnp.einsum('ik,txkz->txiz', cos_y, hat, precision=high)
    next_potential = jnp.einsum('ik,txyk->txyi', cos_z, hat, precision=high)
    return (next_potential, next_multiplier)
```

```python
import math

import jax
import jax.numpy as jnp
import numpy as np
from jax import lax
from jax.experimental import pallas as pl
from jax.experimental.pallas import tpu as pltpu
from jax.sharding import PartitionSpec as P

NEWTON = 10
RATE = 4.0
PROX = 0.01
LANES = 128
GROUP = 8
BATCH = 8
PIECES = 2
VMEM_LIMIT = 56 * 1024 * 1024


def cosine_table(length):
    freq = np.arange(length, dtype=np.float64)[:, None]
    place = np.arange(length, dtype=np.float64)[None, :]
    weight = np.where(freq == 0.0, np.sqrt(0.5), 1.0)
    return np.sqrt(2.0 / length) * weight * np.cos(np.pi * freq * (place + 0.5) / length)


def eigen(length):
    return 4.0 * np.square(np.sin(np.pi * np.arange(length) / (2.0 * length)))


def dct(xs, scale=1.0):
    n = len(xs)
    if n == 1:
        return [xs[0] * scale]
    h = n // 2
    even = dct([xs[i] + xs[n - 1 - i] for i in range(h)], scale * math.sqrt(0.5))
    diff = [xs[i] - xs[n - 1 - i] for i in range(h)]
    out = []
    for k in range(h):
        total = None
        for i in range(h):
            c = scale * math.sqrt(2.0 / n) * math.cos(math.pi * (2 * k + 1) * (i + 0.5) / n)
            term = diff[i] * c
            total = term if total is None else total + term
        out += [even[k], total]
    return out


def halves(x):
    top = x.astype(jnp.bfloat16)
    return top, (x - top.astype(jnp.float32)).astype(jnp.bfloat16)


def right_mm(x, table):
    top, low = halves(x)
    return jnp.dot(jnp.concatenate([top, low, top], axis=1), table, preferred_element_type=jnp.float32)


def left_mm(table, x):
    top, low = halves(x)
    return jnp.dot(table, jnp.concatenate([top, low, top], axis=0), preferred_element_type=jnp.float32)


def plane_mm(planes, left, right):
    n = len(planes)
    size, lanes = planes[0].shape
    half = right_mm(jnp.concatenate(planes, axis=0), right)
    half = jnp.concatenate([half[i * size : (i + 1) * size] for i in range(n)], axis=1)
    full = left_mm(left, half)
    return [full[:, i * lanes : (i + 1) * lanes] for i in range(n)]


def refined(d):
    r = pl.reciprocal(d, approx=True)
    return r * (2.0 - d * r)


def pointwise_kernel(n_in, first_row, lead, count, rows, steps, n_tm, *refs):
    flags, pot, nxt, ht, mult, start, final, cz, cy = refs[:9]
    at_end = first_row + count == rows
    fx_in = None if lead else refs[9]
    hx = refs[9 + (not lead)] if at_end else None
    nm, fx_out = refs[n_in : n_in + 2]
    pay = refs[n_in + 2 : n_in + 2 + n_tm]
    rhs, fx, ft, fyb = refs[n_in + 2 + n_tm :]
    i = pl.program_id(0)
    width = pot.shape[2]
    height = width // PIECES
    block = width // n_tm
    batch = min(BATCH, steps // 2)
    has_t, has_x, first_t, last_t = flags[0, 0], flags[0, 1], flags[0, 2], flags[0, 3]

    @pl.when(i == 0)
    def _():
        fx[...] = jnp.zeros_like(fx) if lead else fx_in[...]
        fyb[...] = jnp.zeros_like(fyb)

    def transform(t, n):
        for k, full in enumerate(plane_mm([rhs[t + k] for k in range(n)], cy[...], cz[...])):
            for d in range(n_tm):
                pay[d][t + k, 0] = full[d * block : (d + 1) * block]

    def plane(t, is_last):
        end_row = i == lead + rows - 1 - first_row
        gate_x = jnp.where(end_row, has_x, 1.0)
        lane = lax.broadcasted_iota(jnp.int32, (height, LANES), 1)
        row = lax.broadcasted_iota(jnp.int32, (height, LANES), 0)
        for part in range(PIECES):
            at = pl.ds(part * height, height)
            p = pot[t, 0, at, :]
            if is_last:
                gt = (ht[0, 0, at, :] - p) * has_t
            else:
                gt = pot[t + 1, 0, at, :] - p
            beside = nxt[t, 0, at, :]
            if at_end:
                beside = jnp.where(end_row, hx[t, 0, at, :], beside)
                gx = (beside - p) * gate_x
            else:
                gx = beside - p
            if part < PIECES - 1:
                gy = pot[t, 0, pl.ds(part * height + 1, height), :] - p
            else:
                gy = jnp.where(row == height - 1, 0.0, pltpu.roll(p, height - 1, 0) - p)
            gz = jnp.where(lane == LANES - 1, 0.0, pltpu.roll(p, LANES - 1, 1) - p)
            a = gt + mult[0, t, 0, at, :] * (1.0 / RATE)
            b1 = gx + mult[1, t, 0, at, :] * (1.0 / RATE)
            b2 = gy + mult[2, t, 0, at, :] * (1.0 / RATE)
            b3 = gz + mult[3, t, 0, at, :] * (1.0 / RATE)
            w = b1 * b1 + b2 * b2 + b3 * b3
            c = a + 1.0
            w15 = 1.5 * w
            s = jnp.maximum(1.0, c)
            for step in range(NEWTON):
                sq = s * s
                d = s * sq + w
                inv = refined(d) if step == NEWTON - 1 else pl.reciprocal(d, approx=True)
                s = jnp.maximum(1.0, s * (c * sq + w15) * inv)
            inside = a + 0.5 * w <= 0.0
            shift = jnp.where(inside, 0.0, s - 1.0)
            k = shift * refined(s)
            k4 = k * RATE
            k8 = k4 * 2.0 - RATE
            nm[0, t, 0, at, :] = shift * RATE
            nm[1, t, 0, at, :] = b1 * k4
            nm[2, t, 0, at, :] = b2 * k4
            nm[3, t, 0, at, :] = b3 * k4
            f0 = shift * (2.0 * RATE) - a * RATE
            f1 = b1 * k8
            f2 = b2 * k8
            f3 = b3 * k8
            if part == PIECES - 1:
                f2 = jnp.where(row == height - 1, 0.0, f2)
            f3 = jnp.where(lane == LANES - 1, 0.0, f3)
            if at_end:
                f1 = f1 * gate_x
            fyb[pl.ds(GROUP + part * height, height), :] = f2
            total = PROX * p + (f1 - fx[t, at, :]) + (f3 - pltpu.roll(f3, 1, 1))
            total = total + (f2 - fyb[pl.ds(GROUP - 1 + part * height, height), :])
            total = total - ft[at, :]
            if is_last:
                total = total - final[0, at, :] * last_t
                rhs[steps, at, :] = f0
            else:
                total = total + f0
                ft[at, :] = f0
            fx[t, at, :] = f1
            rhs[t, at, :] = total

    ft[...] = start[0] * (-first_t)
    for k in range(batch):
        plane(k, False)

    def step_of(b, carry):
        transform((b - 1) * batch, batch)
        for k in range(batch):
            plane(b * batch + k, False)
        return carry

    lax.fori_loop(1, steps // batch - 1, step_of, 0)
    transform(steps - 2 * batch, batch)
    for k in range(batch):
        plane(steps - batch + k, k == batch - 1)
    transform(steps - batch, batch)
    transform(steps, 1)

    @pl.when(i == lead + count - 1)
    def _():
        fx_out[...] = fx[...]


def thirds(table):
    table = np.asarray(table, np.float32)
    top = table.astype(jnp.bfloat16)
    low = (table - top.astype(np.float32)).astype(jnp.bfloat16)
    return jnp.asarray(np.stack([top, top, low]))


def cost(cells, picoseconds):
    return pl.CostEstimate(flops=int(cells * picoseconds * 1150), bytes_accessed=0, transcendentals=0)


def params():
    return pltpu.CompilerParams(vmem_limit_bytes=VMEM_LIMIT)


def pointwise(first_row, lead, count, n_tm, operands, tables, fx_in, nm):
    potential, multiplier = operands[1], operands[2]
    steps, rows, width, _ = potential.shape
    flags, potential, multiplier, start, final, ahead_t, ahead_x = operands
    here = lambda i: jnp.minimum(first_row - lead + i, rows - 1)
    slot = lambda i: jnp.maximum(i - lead, 0)
    plane = (width, LANES)
    block = width // n_tm
    in_specs = [
        pl.BlockSpec(memory_space=pltpu.SMEM),
        pl.BlockSpec((steps, 1) + plane, lambda i: (0, here(i), 0, 0)),
        pl.BlockSpec((steps, 1) + plane, lambda i: (0, here(i + 1), 0, 0)),
        pl.BlockSpec((1, 1) + plane, lambda i: (0, here(i), 0, 0)),
        pl.BlockSpec((4, steps, 1) + plane, lambda i: (0, 0, here(i), 0, 0)),
        pl.BlockSpec((1,) + plane, lambda i: (here(i), 0, 0)),
        pl.BlockSpec((1,) + plane, lambda i: (here(i), 0, 0)),
        pl.BlockSpec((3 * LANES, LANES), lambda i: (0, 0)),
        pl.BlockSpec((width, 3 * width), lambda i: (0, 0)),
    ]
    inputs = [flags, potential, potential, ahead_t, multiplier, start, final, *tables]
    aliases = {}
    if not lead:
        in_specs.append(pl.BlockSpec((steps,) + plane, lambda i: (0, 0, 0)))
        inputs.append(fx_in)
    if first_row + count == rows:
        in_specs.append(pl.BlockSpec((steps, 1) + plane, lambda i: (0, 0, 0, 0)))
        inputs.append(ahead_x)
    if nm is not None:
        in_specs.append(pl.BlockSpec(memory_space=pl.ANY))
        aliases = {len(inputs): 0}
        inputs.append(nm)
    f32 = jnp.float32
    cells = count * steps * width * LANES
    return pl.pallas_call(
        lambda *refs: pointwise_kernel(len(inputs), first_row, lead, count, rows, steps, n_tm, *refs),
        grid=(lead + count,),
        in_specs=in_specs,
        out_specs=[
            pl.BlockSpec((4, steps, 1) + plane, lambda i: (0, 0, first_row + slot(i), 0, 0)),
            pl.BlockSpec((steps,) + plane, lambda i: (0, 0, 0)),
        ]
        + [pl.BlockSpec((steps + 1, 1, block, LANES), lambda i: (0, slot(i), 0, 0))] * n_tm,
        out_shape=[
            jax.ShapeDtypeStruct(multiplier.shape, f32),
            jax.ShapeDtypeStruct((steps,) + plane, f32),
        ]
        + [jax.ShapeDtypeStruct((steps + 1, count, block, LANES), f32)] * n_tm,
        scratch_shapes=[
            pltpu.VMEM((steps + 1,) + plane, f32),
            pltpu.VMEM((steps,) + plane, f32),
            pltpu.VMEM(plane, f32),
            pltpu.VMEM((width + GROUP, LANES), f32),
        ],
        input_output_aliases=aliases,
        compiler_params=params(),
        cost_estimate=cost(cells * (lead + count) // count, 36),
        name="pointwise",
    )(*inputs)


def time_kernel(steps, n_sp, spot, *refs):
    t_all, stage = refs[-2:]
    got, out = refs[: -2 - n_sp], refs[-2 - n_sp : -2]
    n = len(got)
    me_t, me_x = spot[0, 0], spot[0, 1]
    total = n * steps
    share = total // n_sp

    def group(i, carry):
        at = pl.ds(pl.multiple_of(i * GROUP, GROUP), GROUP)
        for d in range(n):
            s = me_t ^ d
            t_all[s, pl.ds(0, steps + 1)] = got[d][:, 0, at, :]
        xs = [t_all[b, t] for b in range(n) for t in range(steps)]
        for b in range(n - 1):
            flux = t_all[b, steps]
            xs[(b + 1) * steps - 1] = xs[(b + 1) * steps - 1] + flux
            xs[(b + 1) * steps] = xs[(b + 1) * steps] - flux
        for k, v in enumerate(dct(xs)):
            stage[(k // share) ^ me_x, k % share] = v
        for d in range(n_sp):
            out[d][:, 0, at, :] = stage[d]
        return carry

    lax.fori_loop(0, got[0].shape[2] // GROUP, group, 0)


def time_transform(spot, got, n_sp):
    planes, count, block, lanes = got[0].shape
    n = len(got)
    share = n * (planes - 1) // n_sp
    return pl.pallas_call(
        lambda *refs: time_kernel(planes - 1, n_sp, *refs),
        grid=(count,),
        in_specs=[pl.BlockSpec(memory_space=pltpu.SMEM)]
        + [pl.BlockSpec((planes, 1, block, lanes), lambda i: (0, i, 0, 0))] * n,
        out_specs=[pl.BlockSpec((share, 1, block, lanes), lambda i: (0, i, 0, 0))] * n_sp,
        out_shape=[jax.ShapeDtypeStruct((share, count, block, lanes), jnp.float32)] * n_sp,
        scratch_shapes=[
            pltpu.VMEM((n, planes, GROUP, lanes), jnp.float32),
            pltpu.VMEM((n_sp, share, GROUP, lanes), jnp.float32),
        ],
        compiler_params=params(),
        cost_estimate=cost(got[0].size * n, 10),
        name="time",
    )(spot, *got)


def middle_kernel(n_sp, first_rows, spot, sig, *refs):
    x_all, stage = refs[-2:]
    got, out = refs[: -2 - n_sp], refs[-2 - n_sp : -2]
    me = spot[0, 1]
    share, count = got[0].shape[:2]
    rows = count * len(first_rows)
    eig = RATE * eigen(rows * n_sp)

    def one(k, carry):
        for c, first in enumerate(first_rows):
            for d in range(n_sp):
                for r in range(count):
                    x_all[d ^ me, first + r] = got[c * n_sp + d][k, r]
        xs = dct([x_all[j, r] for j in range(n_sp) for r in range(rows)])
        base = sig[k]
        xs = [x * refined(base + float(eig[i])) for i, x in enumerate(xs)]
        for x, v in enumerate(dct(xs)):
            stage[(x // rows) ^ me, x % rows] = v
        for d in range(n_sp):
            out[d][k] = stage[d]
        return carry

    lax.fori_loop(0, share, one, 0)


def middle(g, spot, sig, got, first_rows, n_sp):
    share, count, block, lanes = got[0].shape
    rows = count * len(first_rows)
    f32 = jnp.float32
    size = n_sp * share * rows * GROUP * lanes
    return pl.pallas_call(
        lambda *refs: middle_kernel(n_sp, first_rows, *refs),
        grid=(1,),
        in_specs=[
            pl.BlockSpec(memory_space=pltpu.SMEM),
            pl.BlockSpec((share, GROUP, lanes), lambda i: (0, g, 0)),
        ]
        + [pl.BlockSpec((share, count, GROUP, lanes), lambda i: (0, 0, g, 0))] * len(got),
        out_specs=[pl.BlockSpec((share, rows, GROUP, lanes), lambda i: (0, 0, 0, 0))] * n_sp,
        out_shape=[jax.ShapeDtypeStruct((share, rows, GROUP, lanes), f32)] * n_sp,
        scratch_shapes=[pltpu.VMEM((n_sp, rows, GROUP, lanes), f32)] * 2,
        compiler_params=params(),
        cost_estimate=cost(size, 18),
        name="middle",
    )(spot, sig, *got)


def untime_kernel(steps, n_tm, spot, *refs):
    k_all, stage = refs[-2:]
    got, out = refs[: -2 - n_tm], refs[-2 - n_tm : -2]
    me_t, me_x = spot[0, 0], spot[0, 1]
    share, rows = got[0].shape[:2]

    def one(r, carry):
        for d in range(len(got)):
            k_all[d ^ me_x] = got[d][:, r]
        xs = dct([k_all[j, k] for j in range(len(got)) for k in range(share)])
        for t, v in enumerate(xs):
            stage[(t // steps) ^ me_t, t % steps] = v
        for d in range(n_tm):
            out[d][:, r] = stage[d]
        return carry

    lax.fori_loop(0, rows, one, 0)


def untime(spot, got, n_tm):
    share, rows, group, lanes = got[0].shape
    steps = share * len(got) // n_tm
    f32 = jnp.float32
    size = n_tm * steps * rows * group * lanes
    return pl.pallas_call(
        lambda *refs: untime_kernel(steps, n_tm, *refs),
        grid=(1,),
        in_specs=[pl.BlockSpec(memory_space=pltpu.SMEM)]
        + [pl.BlockSpec(got[0].shape, lambda i: (0, 0, 0, 0))] * len(got),
        out_specs=[pl.BlockSpec((steps, rows, group, lanes), lambda i: (0, 0, 0, 0))] * n_tm,
        out_shape=[jax.ShapeDtypeStruct((steps, rows, group, lanes), f32)] * n_tm,
        scratch_shapes=[
            pltpu.VMEM((len(got), share, group, lanes), f32),
            pltpu.VMEM((n_tm, steps, group, lanes), f32),
        ],
        compiler_params=params(),
        cost_estimate=cost(size, 11),
        name="untime",
    )(spot, *got)


def back_kernel(*refs):
    got, (cy, cz, out, whole) = refs[:-4], refs[-4:]
    for t in range(out.shape[0]):
        for n, part in enumerate(got):
            whole[t, pl.ds(n * GROUP, GROUP), :] = part[t, 0]

    batch = min(BATCH, out.shape[0])

    def some(b, carry):
        planes = [whole[b * batch + k] for k in range(batch)]
        for k, full in enumerate(plane_mm(planes, cy[...], cz[...])):
            out[b * batch + k, 0] = full
        return carry

    lax.fori_loop(0, out.shape[0] // batch, some, 0)


def back(got, cy, cz):
    steps, rows, group, lanes = got[0].shape
    width = group * len(got)
    return pl.pallas_call(
        back_kernel,
        grid=(rows,),
        in_specs=[pl.BlockSpec((steps, 1, group, lanes), lambda i: (0, i, 0, 0))] * len(got)
        + [
            pl.BlockSpec((width, 3 * width), lambda i: (0, 0)),
            pl.BlockSpec((3 * lanes, lanes), lambda i: (0, 0)),
        ],
        out_specs=pl.BlockSpec((steps, 1, width, lanes), lambda i: (0, i, 0, 0)),
        out_shape=jax.ShapeDtypeStruct((steps, rows, width, lanes), jnp.float32),
        scratch_shapes=[pltpu.VMEM((steps, width, lanes), jnp.float32)],
        compiler_params=params(),
        cost_estimate=cost(steps * rows * width * lanes, 7),
        name="back",
    )(*got, cy, cz)


def from_behind(block, axis, distance):
    devices = range(lax.axis_size(axis))
    route = [(i - distance, i) for i in devices if i - distance in devices]
    return lax.ppermute(block, axis, route)


def trade(parts, axis):
    devices = range(lax.axis_size(axis))
    return [parts[0]] + [
        lax.ppermute(parts[d], axis, [(i, i ^ d) for i in devices]) for d in range(1, len(parts))
    ]


def body(potential, multiplier, start_density, final_density):
    steps, rows, width, lanes = potential.shape
    n_tm = lax.axis_size("tm")
    n_sp = lax.axis_size("space")
    me_t = lax.axis_index("tm")
    me_x = lax.axis_index("space")
    total_t = steps * n_tm
    block = width // n_tm
    groups = block // GROUP
    share = total_t // n_sp
    parts = min(rows, 4)
    count = rows // parts
    f32 = jnp.float32
    ahead_t = from_behind(potential[:1], "tm", -1)
    ahead_x = from_behind(potential[:, :1], "space", -1)
    flags = jnp.stack(
        [me_t < n_tm - 1, me_x < n_sp - 1, me_t == 0, me_t == n_tm - 1]
    ).astype(f32)[None]
    spot = jnp.stack([me_t, me_x]).astype(jnp.int32)[None]

    cos_y = thirds(cosine_table(width))
    to = me_t ^ jnp.arange(n_tm)
    rows_y = cos_y.reshape(3, n_tm, block, width)[:, to].reshape(3, width, width)
    rows_y = rows_y.transpose(1, 0, 2).reshape(width, 3 * width)
    columns_y = cos_y.reshape(3, width, n_tm, groups, GROUP)[:, :, to]
    columns_y = columns_y.transpose(1, 0, 3, 2, 4).reshape(width, 3 * width)
    cos_z = thirds(cosine_table(lanes).T).reshape(3 * lanes, lanes)
    tables = (cos_z, rows_y)

    eig_t = jnp.asarray(eigen(total_t), f32)
    eig_t = lax.dynamic_slice_in_dim(eig_t, me_x * share, share, 0)[:, None, None]
    eig_yz = jnp.asarray(eigen(width)[:, None] + eigen(lanes)[None, :], f32)
    eig_yz = lax.dynamic_slice_in_dim(eig_yz, me_t * block, block, 0)[None]
    sig = RATE * (eig_t + eig_yz) + PROX

    operands = (flags, potential, multiplier, start_density, final_density, ahead_t, ahead_x)
    flux, next_multiplier = None, None
    moved, first_rows = [], []
    for n in range(parts):
        first = ((n + 1) % parts) * count
        if first == 0:
            flux = from_behind(flux, "space", 1)
        next_multiplier, flux, *pay = pointwise(
            first, 1 if n == 0 else 0, count, n_tm, operands, tables, flux, next_multiplier
        )
        timed = time_transform(spot, trade(pay, "tm"), n_sp)
        moved += trade(timed, "space")
        first_rows.append(first)
    final = []
    for g in range(groups):
        solved = middle(g, spot, sig, moved, first_rows, n_sp)
        solved = trade(solved, "space")
        steps_of = untime(spot, solved, n_tm)
        final += trade(steps_of, "tm")
    next_potential = back(final, columns_y, cos_z)
    return (next_potential, next_multiplier)


def solution(mesh):
    in_specs = (
        P("tm", "space", None, None),
        P(None, "tm", "space", None, None),
        P("space", None, None),
        P("space", None, None),
    )
    out_specs = (P("tm", "space", None, None), P(None, "tm", "space", None, None))
    return jax.shard_map(body, mesh=mesh, in_specs=in_specs, out_specs=out_specs, check_vma=False)
```

```python
import math

import jax
import jax.numpy as jnp
import numpy as np
from jax import lax
from jax.experimental import pallas as pl
from jax.experimental.pallas import tpu as pltpu
from jax.sharding import PartitionSpec as P

NEWTON = 10
RATE = 4.0
PROX = 0.01
LANES = 128
GROUP = 8
BATCH = 8
PIECES = 2
VMEM_LIMIT = 56 * 1024 * 1024


def cosine_table(length):
    freq = np.arange(length, dtype=np.float64)[:, None]
    place = np.arange(length, dtype=np.float64)[None, :]
    weight = np.where(freq == 0.0, np.sqrt(0.5), 1.0)
    return np.sqrt(2.0 / length) * weight * np.cos(np.pi * freq * (place + 0.5) / length)


def eigen(length):
    return 4.0 * np.square(np.sin(np.pi * np.arange(length) / (2.0 * length)))


def dct(xs, scale=1.0):
    n = len(xs)
    if n == 1:
        return [xs[0] * scale]
    h = n // 2
    even = dct([xs[i] + xs[n - 1 - i] for i in range(h)], scale * math.sqrt(0.5))
    diff = [xs[i] - xs[n - 1 - i] for i in range(h)]
    out = []
    for k in range(h):
        total = None
        for i in range(h):
            c = scale * math.sqrt(2.0 / n) * math.cos(math.pi * (2 * k + 1) * (i + 0.5) / n)
            term = diff[i] * c
            total = term if total is None else total + term
        out += [even[k], total]
    return out


def halves(x):
    top = x.astype(jnp.bfloat16)
    return top, (x - top.astype(jnp.float32)).astype(jnp.bfloat16)


def right_mm(x, table):
    top, low = halves(x)
    return jnp.dot(jnp.concatenate([top, low, top], axis=1), table, preferred_element_type=jnp.float32)


def left_mm(table, x):
    top, low = halves(x)
    return jnp.dot(table, jnp.concatenate([top, low, top], axis=0), preferred_element_type=jnp.float32)


def plane_mm(planes, left, right):
    n = len(planes)
    size, lanes = planes[0].shape
    half = right_mm(jnp.concatenate(planes, axis=0), right)
    half = jnp.concatenate([half[i * size : (i + 1) * size] for i in range(n)], axis=1)
    full = left_mm(left, half)
    return [full[:, i * lanes : (i + 1) * lanes] for i in range(n)]


def refined(d):
    r = pl.reciprocal(d, approx=True)
    return r * (2.0 - d * r)


def pointwise_kernel(n_in, first_row, lead, count, rows, steps, n_tm, *refs):
    flags, pot, nxt, ht, mult, start, final, cz, cy = refs[:9]
    at_end = first_row + count == rows
    fx_in = None if lead else refs[9]
    hx = refs[9 + (not lead)] if at_end else None
    nm, fx_out = refs[n_in : n_in + 2]
    pay = refs[n_in + 2 : n_in + 2 + n_tm]
    rhs, fx, ft, fyb = refs[n_in + 2 + n_tm :]
    i = pl.program_id(0)
    width = pot.shape[2]
    height = width // PIECES
    block = width // n_tm
    batch = min(BATCH, steps // 2)
    has_t, has_x, first_t, last_t = flags[0, 0], flags[0, 1], flags[0, 2], flags[0, 3]

    @pl.when(i == 0)
    def _():
        fx[...] = jnp.zeros_like(fx) if lead else fx_in[...]
        fyb[...] = jnp.zeros_like(fyb)

    def transform(t, n):
        for k, full in enumerate(plane_mm([rhs[t + k] for k in range(n)], cy[...], cz[...])):
            for d in range(n_tm):
                pay[d][t + k, 0] = full[d * block : (d + 1) * block]

    def plane(t, is_last):
        end_row = i == lead + rows - 1 - first_row
        gate_x = jnp.where(end_row, has_x, 1.0)
        lane = lax.broadcasted_iota(jnp.int32, (height, LANES), 1)
        row = lax.broadcasted_iota(jnp.int32, (height, LANES), 0)
        for part in range(PIECES):
            at = pl.ds(part * height, height)
            p = pot[t, 0, at, :]
            if is_last:
                gt = (ht[0, 0, at, :] - p) * has_t
            else:
                gt = pot[t + 1, 0, at, :] - p
            beside = nxt[t, 0, at, :]
            if at_end:
                beside = jnp.where(end_row, hx[t, 0, at, :], beside)
                gx = (beside - p) * gate_x
            else:
                gx = beside - p
            if part < PIECES - 1:
                gy = pot[t, 0, pl.ds(part * height + 1, height), :] - p
            else:
                gy = jnp.where(row == height - 1, 0.0, pltpu.roll(p, height - 1, 0) - p)
            gz = jnp.where(lane == LANES - 1, 0.0, pltpu.roll(p, LANES - 1, 1) - p)
            a = gt + mult[0, t, 0, at, :] * (1.0 / RATE)
            b1 = gx + mult[1, t, 0, at, :] * (1.0 / RATE)
            b2 = gy + mult[2, t, 0, at, :] * (1.0 / RATE)
            b3 = gz + mult[3, t, 0, at, :] * (1.0 / RATE)
            w = b1 * b1 + b2 * b2 + b3 * b3
            c = a + 1.0
            w15 = 1.5 * w
            s = jnp.maximum(1.0, c)
            for step in range(NEWTON):
                sq = s * s
                d = s * sq + w
                inv = refined(d) if step == NEWTON - 1 else pl.reciprocal(d, approx=True)
                s = jnp.maximum(1.0, s * (c * sq + w15) * inv)
            inside = a + 0.5 * w <= 0.0
            shift = jnp.where(inside, 0.0, s - 1.0)
            k = shift * refined(s)
            k4 = k * RATE
            k8 = k4 * 2.0 - RATE
            nm[0, t, 0, at, :] = shift * RATE
            nm[1, t, 0, at, :] = b1 * k4
            nm[2, t, 0, at, :] = b2 * k4
            nm[3, t, 0, at, :] = b3 * k4
            f0 = shift * (2.0 * RATE) - a * RATE
            f1 = b1 * k8
            f2 = b2 * k8
            f3 = b3 * k8
            if part == PIECES - 1:
                f2 = jnp.where(row == height - 1, 0.0, f2)
            f3 = jnp.where(lane == LANES - 1, 0.0, f3)
            if at_end:
                f1 = f1 * gate_x
            fyb[pl.ds(GROUP + part * height, height), :] = f2
            total = PROX * p + (f1 - fx[t, at, :]) + (f3 - pltpu.roll(f3, 1, 1))
            total = total + (f2 - fyb[pl.ds(GROUP - 1 + part * height, height), :])
            total = total - ft[at, :]
            if is_last:
                total = total - final[0, at, :] * last_t
                rhs[steps, at, :] = f0
            else:
                total = total + f0
                ft[at, :] = f0
            fx[t, at, :] = f1
            rhs[t, at, :] = total

    ft[...] = start[0] * (-first_t)
    for k in range(batch):
        plane(k, False)

    def step_of(b, carry):
        transform((b - 1) * batch, batch)
        for k in range(batch):
            plane(b * batch + k, False)
        return carry

    lax.fori_loop(1, steps // batch - 1, step_of, 0)
    transform(steps - 2 * batch, batch)
    for k in range(batch):
        plane(steps - batch + k, k == batch - 1)
    transform(steps - batch, batch)
    transform(steps, 1)

    @pl.when(i == lead + count - 1)
    def _():
        fx_out[...] = fx[...]


def thirds(table):
    table = np.asarray(table, np.float32)
    top = table.astype(jnp.bfloat16)
    low = (table - top.astype(np.float32)).astype(jnp.bfloat16)
    return jnp.asarray(np.stack([top, top, low]))


def cost(cells, picoseconds):
    return pl.CostEstimate(flops=int(cells * picoseconds * 500), bytes_accessed=0, transcendentals=0)


def params():
    return pltpu.CompilerParams(vmem_limit_bytes=VMEM_LIMIT)


def pointwise(first_row, lead, count, n_tm, operands, tables, fx_in, nm):
    potential, multiplier = operands[1], operands[2]
    steps, rows, width, _ = potential.shape
    flags, potential, multiplier, start, final, (from_row, ahead_t), ahead_x = operands
    here = lambda i: jnp.minimum(first_row - lead + i, rows - 1)
    slot = lambda i: jnp.maximum(i - lead, 0)
    plane = (width, LANES)
    block = width // n_tm
    in_specs = [
        pl.BlockSpec(memory_space=pltpu.SMEM),
        pl.BlockSpec((steps, 1) + plane, lambda i: (0, here(i), 0, 0)),
        pl.BlockSpec((steps, 1) + plane, lambda i: (0, here(i + 1), 0, 0)),
        pl.BlockSpec((1, 1) + plane, lambda i: (0, here(i) - from_row, 0, 0)),
        pl.BlockSpec((4, steps, 1) + plane, lambda i: (0, 0, here(i), 0, 0)),
        pl.BlockSpec((1,) + plane, lambda i: (here(i), 0, 0)),
        pl.BlockSpec((1,) + plane, lambda i: (here(i), 0, 0)),
        pl.BlockSpec((3 * LANES, LANES), lambda i: (0, 0)),
        pl.BlockSpec((width, 3 * width), lambda i: (0, 0)),
    ]
    inputs = [flags, potential, potential, ahead_t, multiplier, start, final, *tables]
    aliases = {}
    if not lead:
        in_specs.append(pl.BlockSpec((steps,) + plane, lambda i: (0, 0, 0)))
        inputs.append(fx_in)
    if first_row + count == rows:
        in_specs.append(pl.BlockSpec((steps, 1) + plane, lambda i: (0, 0, 0, 0)))
        inputs.append(ahead_x)
    if nm is not None:
        in_specs.append(pl.BlockSpec(memory_space=pl.ANY))
        aliases = {len(inputs): 0}
        inputs.append(nm)
    f32 = jnp.float32
    cells = count * steps * width * LANES
    return pl.pallas_call(
        lambda *refs: pointwise_kernel(len(inputs), first_row, lead, count, rows, steps, n_tm, *refs),
        grid=(lead + count,),
        in_specs=in_specs,
        out_specs=[
            pl.BlockSpec((4, steps, 1) + plane, lambda i: (0, 0, first_row + slot(i), 0, 0)),
            pl.BlockSpec((steps,) + plane, lambda i: (0, 0, 0)),
        ]
        + [pl.BlockSpec((steps + 1, 1, block, LANES), lambda i: (0, slot(i), 0, 0))] * n_tm,
        out_shape=[
            jax.ShapeDtypeStruct(multiplier.shape, f32),
            jax.ShapeDtypeStruct((steps,) + plane, f32),
        ]
        + [jax.ShapeDtypeStruct((steps + 1, count, block, LANES), f32)] * n_tm,
        scratch_shapes=[
            pltpu.VMEM((steps + 1,) + plane, f32),
            pltpu.VMEM((steps,) + plane, f32),
            pltpu.VMEM(plane, f32),
            pltpu.VMEM((width + GROUP, LANES), f32),
        ],
        input_output_aliases=aliases,
        compiler_params=params(),
        cost_estimate=cost(cells * (lead + count) // count, 36),
        name="pointwise",
    )(*inputs)


def time_kernel(steps, n_sp, spot, *refs):
    got, (out, t_all) = refs[:-2], refs[-2:]
    n = len(got)
    me_t = spot[0, 0]
    total = n * steps
    share = total // n_sp

    def group(i, carry):
        at = pl.ds(pl.multiple_of(i * GROUP, GROUP), GROUP)
        for d in range(n):
            s = me_t ^ d
            t_all[s, pl.ds(0, steps + 1)] = got[d][:, 0, at, :]
        xs = [t_all[b, t] for b in range(n) for t in range(steps)]
        for b in range(n - 1):
            flux = t_all[b, steps]
            xs[(b + 1) * steps - 1] = xs[(b + 1) * steps - 1] + flux
            xs[(b + 1) * steps] = xs[(b + 1) * steps] - flux
        for k, v in enumerate(dct(xs)):
            out[k // share, k % share, 0, at, :] = v
        return carry

    lax.fori_loop(0, got[0].shape[2] // GROUP, group, 0)


def time_transform(spot, got, n_sp):
    planes, count, block, lanes = got[0].shape
    n = len(got)
    share = n * (planes - 1) // n_sp
    return pl.pallas_call(
        lambda *refs: time_kernel(planes - 1, n_sp, *refs),
        grid=(count,),
        in_specs=[pl.BlockSpec(memory_space=pltpu.SMEM)]
        + [pl.BlockSpec((planes, 1, block, lanes), lambda i: (0, i, 0, 0))] * n,
        out_specs=pl.BlockSpec((n_sp, share, 1, block, lanes), lambda i: (0, 0, i, 0, 0)),
        out_shape=jax.ShapeDtypeStruct((n_sp, share, count, block, lanes), jnp.float32),
        scratch_shapes=[pltpu.VMEM((n, planes, GROUP, lanes), jnp.float32)],
        compiler_params=params(),
        cost_estimate=cost(got[0].size * n, 10),
        name="time",
    )(spot, *got)


def middle_kernel(n_sp, first_rows, sig, *refs):
    got, outs = refs[: len(first_rows)], refs[len(first_rows) :]
    share = got[0].shape[1]
    rows = sum(part.shape[2] for part in got)
    each = rows // len(outs)
    eig = RATE * eigen(rows * n_sp)
    parts = sorted(zip(first_rows, got), key=lambda part: part[0])

    def one(k, carry):
        xs = dct([part[j, k, r] for j in range(n_sp) for _, part in parts for r in range(part.shape[2])])
        base = sig[k]
        xs = [x * refined(base + float(eig[i])) for i, x in enumerate(xs)]
        for x, v in enumerate(dct(xs)):
            r = x % rows
            outs[r // each][x // rows, k, r % each] = v
        return carry

    lax.fori_loop(0, share, one, 0)


def middle(g, sig, got, first_rows, pieces):
    n_sp, share, _, block, lanes = got[0].shape
    rows = sum(part.shape[2] for part in got)
    out = (n_sp, share, rows // pieces, GROUP, lanes)
    return pl.pallas_call(
        lambda *refs: middle_kernel(n_sp, first_rows, *refs),
        grid=(1,),
        in_specs=[pl.BlockSpec((share, GROUP, lanes), lambda i: (0, g, 0))]
        + [
            pl.BlockSpec(part.shape[:3] + (GROUP, lanes), lambda i: (0, 0, 0, g, 0)) for part in got
        ],
        out_specs=[pl.BlockSpec(out, lambda i: (0, 0, 0, 0, 0))] * pieces,
        out_shape=[jax.ShapeDtypeStruct(out, jnp.float32)] * pieces,
        compiler_params=params(),
        cost_estimate=cost(math.prod(out) * pieces, 18),
        name="middle",
    )(sig, *got)


def untime_kernel(steps, n_tm, spot, got, *refs):
    out, stage = refs[:-1], refs[-1]
    me_t = spot[0, 0]
    n, share, rows = got.shape[:3]

    def one(r, carry):
        xs = dct([got[j, k, r] for j in range(n) for k in range(share)])
        for t, v in enumerate(xs):
            stage[(t // steps) ^ me_t, t % steps] = v
        for d in range(n_tm):
            out[d][:, r] = stage[d]
        return carry

    lax.fori_loop(0, rows, one, 0)


def untime(spot, got, n_tm):
    n_sp, share, rows, group, lanes = got.shape
    steps = share * n_sp // n_tm
    f32 = jnp.float32
    return pl.pallas_call(
        lambda *refs: untime_kernel(steps, n_tm, *refs),
        grid=(1,),
        in_specs=[
            pl.BlockSpec(memory_space=pltpu.SMEM),
            pl.BlockSpec(got.shape, lambda i: (0, 0, 0, 0, 0)),
        ],
        out_specs=[pl.BlockSpec((steps, rows, group, lanes), lambda i: (0, 0, 0, 0))] * n_tm,
        out_shape=[jax.ShapeDtypeStruct((steps, rows, group, lanes), f32)] * n_tm,
        scratch_shapes=[pltpu.VMEM((n_tm, steps, group, lanes), f32)],
        compiler_params=params(),
        cost_estimate=cost(got.size, 11),
        name="untime",
    )(spot, got)


def back_kernel(n_got, *refs):
    got, cy, cz = refs[:n_got], refs[n_got], refs[n_got + 1]
    out, whole = refs[-2:]
    batch = min(BATCH, out.shape[0])
    for t in range(out.shape[0]):
        for n, part in enumerate(got):
            whole[t, pl.ds(n * GROUP, GROUP), :] = part[t, 0]

    def some(b, carry):
        planes = [whole[b * batch + k] for k in range(batch)]
        for k, full in enumerate(plane_mm(planes, cy[...], cz[...])):
            out[b * batch + k, 0] = full
        return carry

    lax.fori_loop(0, out.shape[0] // batch, some, 0)


def back(first, count, rows, got, cy, cz, result):
    steps, _, group, lanes = got[0][1].shape
    width = group * len(got)
    in_specs = [
        pl.BlockSpec((steps, 1, group, lanes), lambda i, skip=first - at: (0, i + skip, 0, 0)) for at, _ in got
    ] + [
        pl.BlockSpec((width, 3 * width), lambda i: (0, 0)),
        pl.BlockSpec((3 * lanes, lanes), lambda i: (0, 0)),
    ]
    inputs = [part for _, part in got] + [cy, cz]
    aliases = {}
    if result is not None:
        in_specs.append(pl.BlockSpec(memory_space=pl.ANY))
        aliases = {len(inputs): 0}
        inputs.append(result)
    return pl.pallas_call(
        lambda *refs: back_kernel(len(got), *refs),
        grid=(count,),
        in_specs=in_specs,
        out_specs=pl.BlockSpec((steps, 1, width, lanes), lambda i: (0, first + i, 0, 0)),
        out_shape=jax.ShapeDtypeStruct((steps, rows, width, lanes), jnp.float32),
        scratch_shapes=[pltpu.VMEM((steps, width, lanes), jnp.float32)],
        input_output_aliases=aliases,
        compiler_params=params(),
        cost_estimate=cost(steps * count * width * lanes, 7),
        name="back",
    )(*inputs)


def from_behind(block, axis, distance):
    devices = range(lax.axis_size(axis))
    route = [(i - distance, i) for i in devices if i - distance in devices]
    return lax.ppermute(block, axis, route)


def trade(parts, axis):
    devices = range(lax.axis_size(axis))
    return [parts[0]] + [
        lax.ppermute(parts[d], axis, [(i, i ^ d) for i in devices]) for d in range(1, len(parts))
    ]


def swap(parts):
    return lax.all_to_all(parts, "space", split_axis=0, concat_axis=0, tiled=True)


def body(potential, multiplier, start_density, final_density):
    steps, rows, width, lanes = potential.shape
    n_tm = lax.axis_size("tm")
    n_sp = lax.axis_size("space")
    me_t = lax.axis_index("tm")
    me_x = lax.axis_index("space")
    total_t = steps * n_tm
    block = width // n_tm
    groups = block // GROUP
    share = total_t // n_sp
    size = 2 if rows > 4 and rows % 2 == 0 else 1
    inner = [1 + size * n for n in range((rows - 2) // size)]
    firsts = [1, rows - 1] + inner[1:] + [0]
    counts = [size, 1] + [size] * (len(inner) - 1) + [1]
    leads = [1, 1] + [0] * (len(counts) - 2)
    f32 = jnp.float32
    early = size + 1
    ahead_t = (0, from_behind(potential[:1, :early], "tm", -1))
    ahead_rest = (early, from_behind(potential[:1, early:], "tm", -1))
    ahead_x = from_behind(potential[:, :1], "space", -1)
    flags = jnp.stack(
        [me_t < n_tm - 1, me_x < n_sp - 1, me_t == 0, me_t == n_tm - 1]
    ).astype(f32)[None]
    spot = jnp.stack([me_t, me_x]).astype(jnp.int32)[None]

    cos_y = thirds(cosine_table(width))
    to = me_t ^ jnp.arange(n_tm)
    rows_y = cos_y.reshape(3, n_tm, block, width)[:, to].reshape(3, width, width)
    rows_y = rows_y.transpose(1, 0, 2).reshape(width, 3 * width)
    columns_y = cos_y.reshape(3, width, n_tm, groups, GROUP)[:, :, to]
    columns_y = columns_y.transpose(1, 0, 3, 2, 4).reshape(width, 3 * width)
    cos_z = thirds(cosine_table(lanes).T).reshape(3 * lanes, lanes)
    tables = (cos_z, rows_y)

    eig_t = jnp.asarray(eigen(total_t), f32)
    eig_t = lax.dynamic_slice_in_dim(eig_t, me_x * share, share, 0)[:, None, None]
    eig_yz = jnp.asarray(eigen(width)[:, None] + eigen(lanes)[None, :], f32)
    eig_yz = lax.dynamic_slice_in_dim(eig_yz, me_t * block, block, 0)[None]
    sig = RATE * (eig_t + eig_yz) + PROX

    flux, next_multiplier = None, None
    ready, moved, waiting, behind = [], [], None, None
    for n, (first, count, lead) in enumerate(zip(firsts, counts, leads)):
        operands = (
            flags, potential, multiplier, start_density, final_density,
            ahead_t if first < early else ahead_rest, ahead_x,
        )
        next_multiplier, new_flux, *pay = pointwise(
            first, lead, count, n_tm, operands, tables, flux if first else behind, next_multiplier
        )
        if first == rows - 1:
            behind = new_flux
        else:
            flux = new_flux
        if n == 2:
            behind, _, _ = lax.optimization_barrier((behind, moved[0], pay[0]))
            behind = from_behind(behind, "space", 1)
        if n:
            waiting, next_multiplier = lax.optimization_barrier((waiting, next_multiplier))
            ready.append(time_transform(spot, waiting, n_sp))
            _, next_multiplier = lax.optimization_barrier((ready[-1], next_multiplier))
        if n == 1:
            moved.append(swap(ready[0]))
        waiting = trade(pay, "tm")
    ready.append(time_transform(spot, waiting, n_sp))

    for n, timed in enumerate(ready):
        if n == 0:
            continue
        if n == 1:
            timed, _ = lax.optimization_barrier((timed, behind))
        if n == len(ready) - 2:
            timed, _ = lax.optimization_barrier((timed, ready[-1]))
        timed, _ = lax.optimization_barrier((timed, moved[-1]))
        moved.append(swap(timed))

    pieces = 2 if rows % 2 == 0 else 1
    solved = []
    for g in range(groups):
        solved += middle(g, sig, moved, firsts, pieces if g == groups - 1 else 1)
    final, done, back_x = [], [], []
    for n, part in enumerate(solved):
        if n:
            part, _ = lax.optimization_barrier((part, back_x[-1]))
        if n + 1 < len(solved) and n >= 2:
            part, final[n - 2] = lax.optimization_barrier((part, final[n - 2]))
        elif n >= 2:
            part, _ = lax.optimization_barrier((part, done[n - 2]))
        part = swap(part)
        back_x.append(part)
        if n + 1 == len(solved) and n >= 2:
            part, final[n - 2] = lax.optimization_barrier((part, final[n - 2]))
        done.append(untime(spot, part, n_tm))
        final.append(trade(done[-1], "tm"))
    next_potential = None
    size = rows // pieces
    for piece in range(pieces):
        got = [(0, part) for some in final[: groups - 1] for part in some]
        got += [(piece * size, part) for part in final[groups - 1 + piece]]
        next_potential = back(piece * size, size, rows, got, columns_y, cos_z, next_potential)
    return (next_potential, next_multiplier)


def solution(mesh):
    in_specs = (
        P("tm", "space", None, None),
        P(None, "tm", "space", None, None),
        P("space", None, None),
        P("space", None, None),
    )
    out_specs = (P("tm", "space", None, None), P(None, "tm", "space", None, None))
    return jax.shard_map(body, mesh=mesh, in_specs=in_specs, out_specs=out_specs, check_vma=False)
```
